32 devices in a mesh: groups: 2 (over x), row: 8 (over z, y), col: 2 (over core).
Axes of the slice: x: 2, y: 2, z: 4, core: 2. Of those that a mesh axis runs over, the one named last changes fastest.
Arguments:
- probes: bfloat16 [4, 32, 32768], P(('groups', 'col'), None, 'row'), parts along dimension 0, may hold values from -6 to 6
- tile_data: bfloat16 [16, 2, 96, 256, 256], P(('groups', 'row'), 'col'), parts along dimension 0, may hold values from -0.09375 to 0.09375
- tile_rows: int32 [16, 2, 96], P(('groups', 'row'), 'col'), parts along dimension 0, may hold values from 0 to 7, as said below
- tile_cols: int32 [16, 2, 96], P(('groups', 'row'), 'col'), parts along dimension 0, may hold values from 0 to 127, as said below
- tile_count: int32 [16, 2, 1], P(('groups', 'row'), 'col'), parts along dimension 0, may hold values from 24 to 96, as said below
- active: int32 [32768], P(('groups', 'row')), parts along dimension 0, may hold values 0 or 1
Outputs:
- newton_image: float32 [4, 32, 32768], P(('groups', 'col'), None, 'row'), parts along dimension 0
The draws below stay inside these ranges and needn't reach their ends.
There are 2 independent parts, one for each index of `groups`. The reference program is written for one: setup_inputs(seed, part) draws one part's arguments, and reference() takes and returns one part's arrays. A program takes and returns all parts, laid end to end along the dimension named above; each array names one. Nothing has to cross between parts.
Inputs may be any that keep to these rules, and one draw needn't show every extreme that they name: `tile_rows`: values index a device's 8 row blocks; the (row block, column block) pairs of one device's 96 slots are all distinct. `tile_cols`: values index the 128 column blocks of the device's column group. The live slots of a device are its first tile_count slots; in every part some device has all 96 slots live.
All inputs are finite; a program needn't handle non-finite values. No bound on the sum of `active` on one device may be relied on, other than what follows from the above.
Results may differ from the reference program's by a relative error of at most 0.001.
Values may be sent and summed in bfloat16 or wider, within the bound.
A program may use at most 64 MiB of HBM per device.

```python
import jax
import jax.numpy as jnp
from jax import lax

TS = 256
PROBES = 32
RBD = 8
CBG = 128
TSLOT = 96
GROUP_COLS = 32768
NROW = 16384
N_ROW = 8
N_COL = 2


def slot_table(key):
    keys = jax.random.split(key, N_ROW * N_COL)
    perms = jax.vmap(lambda single: jax.random.permutation(single, RBD * CBG))(keys)[:, :TSLOT]
    return perms.reshape(N_ROW, N_COL, TSLOT).astype(jnp.int32)


def draw_tile_rows(key, part):
    return (slot_table(key) // CBG).astype(jnp.int32)


def draw_tile_cols(key, part):
    return (slot_table(key) % CBG).astype(jnp.int32)


def draw_tile_count(key, part):
    key = jax.random.fold_in(key, 5)
    first_key, second_key = jax.random.split(key)
    counts = jax.random.randint(first_key, (N_ROW * N_COL,), TSLOT // 4, TSLOT + 1)
    fullest = jax.random.randint(second_key, (), 0, N_ROW * N_COL)
    counts = jnp.where(jnp.arange(N_ROW * N_COL) == fullest, TSLOT, counts)
    return counts.reshape(N_ROW, N_COL, 1).astype(jnp.int32)


def touch_ends(values, key, smallest, high):
    longest = values.shape.index(max(values.shape))
    spots = []
    for shift in (0, 1):
        where = [jax.random.randint(jax.random.fold_in(key, axis), (), 0, length) for axis, length in enumerate(values.shape)]
        where[longest] = (where[longest] + shift) % values.shape[longest]
        spots.append(tuple(where))
    return values.at[spots[0]].set(smallest).at[spots[1]].set(high)


def block_levels(rng, shape, shards, low, high):
    level = 1.0
    for axis_at, shards_of in shards:
        heights = jax.random.uniform(jax.random.fold_in(jax.random.fold_in(rng, 6), axis_at), (shards_of,), jnp.float32, low / len(shards), high / len(shards))
        level = level * jnp.repeat(jnp.exp(heights), shape[axis_at] // shards_of).reshape((-1,) + (1,) * (len(shape) - 1 - axis_at))
    return level


def centred(stream_key, shape, deviation, bound, pieces=(), held_as=jnp.bfloat16):
    array = deviation * jax.random.normal(stream_key, shape, jnp.float32)
    if pieces:
        array = array * block_levels(stream_key, shape, pieces, -0.22, 0.18)
    return jnp.clip(array, -bound, bound).astype(held_as)


def setup_inputs(seed: int = 0, part: int = 0) -> dict:
    splits = jax.random.split(jax.random.key(seed), 7)
    part_splits = jax.random.split(jax.random.fold_in(splits[6], part), 7)
    return {
        "probes": centred(part_splits[0], (N_COL, PROBES, GROUP_COLS), 1.0, 6.0, ((0, 2), (2, 8))),
        "tile_data": centred(part_splits[1], (N_ROW, N_COL, TSLOT, TS, TS), (16 * TS) ** -0.5, 0.09375, ((0, 8), (1, 2))),
        "tile_rows": draw_tile_rows(jax.random.fold_in(jax.random.fold_in(splits[6], part), 71), part),
        "tile_cols": draw_tile_cols(jax.random.fold_in(jax.random.fold_in(splits[6], part), 71), part),
        "tile_count": draw_tile_count(jax.random.fold_in(jax.random.fold_in(splits[6], part), 71), part),
        "active": touch_ends((jax.random.randint(part_splits[5], (NROW,), 0, 5) < 3).astype(jnp.int32), jax.random.fold_in(part_splits[5], 1), 0, 1),
    }


def forward_device(tiles, slot_rows, slot_cols, live_count, vectors):
    live_slots = jnp.arange(TSLOT) < live_count
    row_onehot = ((slot_rows[None, :] == jnp.arange(RBD)[:, None]) & live_slots[None, :]).astype(jnp.float32)
    picked = vectors.reshape(PROBES, CBG, TS)[:, slot_cols]
    products = jnp.einsum('psi,sri->spr', picked.astype(jnp.float32), tiles.astype(jnp.float32), precision=lax.Precision.HIGHEST)
    summed = jnp.einsum('bs,spr->pbr', row_onehot, products, precision=lax.Precision.HIGHEST)
    return summed.reshape(PROBES, RBD * TS)


def backward_device(tiles, slot_rows, slot_cols, live_count, weighted):
    live_slots = jnp.arange(TSLOT) < live_count
    col_onehot = ((slot_cols[None, :] == jnp.arange(CBG)[:, None]) & live_slots[None, :]).astype(jnp.float32)
    masked_rows = weighted.reshape(PROBES, RBD, TS)[:, slot_rows]
    products = jnp.einsum('psr,sri->spi', masked_rows.astype(jnp.float32), tiles.astype(jnp.float32), precision=lax.Precision.HIGHEST)
    summed = jnp.einsum('cs,spi->pci', col_onehot, products, precision=lax.Precision.HIGHEST)
    return summed.reshape(PROBES, CBG * TS)


def reference(probes, tile_data, tile_rows, tile_cols, tile_count, active):
    masks = active.reshape(N_ROW, RBD * TS)

    def one_row(carry, inputs):
        tiles, slot_rows, slot_cols, counts, row_mask = inputs
        partial_value = jax.vmap(forward_device)(tiles, slot_rows, slot_cols, counts[:, 0], probes)
        row_sum = jnp.sum(partial_value, axis=0)
        weighted = (row_sum * row_mask.astype(jnp.float32)[None, :]).astype(jnp.bfloat16)
        back_terms = jax.vmap(backward_device, in_axes=(0, 0, 0, 0, None))(tiles, slot_rows, slot_cols, counts[:, 0], weighted)
        return carry + back_terms, None

    start = jnp.zeros((N_COL, PROBES, GROUP_COLS), jnp.float32)
    total, unused = lax.scan(one_row, start, (tile_data, tile_rows, tile_cols, tile_count, masks))
    return probes.astype(jnp.float32) + total
```

```python
import functools

import jax
import jax.numpy as jnp
from jax import lax
from jax.experimental import pallas as pl
from jax.experimental.pallas import tpu as pltpu
from jax.sharding import PartitionSpec as P

MESH = pl.DeviceIdType.MESH
LEVELS = 32000.0
STEPS = 256.0
TINY = 1e-30


def combine(table_ref, terms, dest, blocks, row_blocks, out):
    def body(j, peak):
        first = (dest * blocks + j) * row_blocks
        total = terms[table_ref[first]]
        for k in range(1, row_blocks):
            total = total + terms[table_ref[first + k]]
        out[j] = total
        return jnp.maximum(peak, jnp.abs(total))

    return lax.fori_loop(0, blocks, body, jnp.zeros(out.shape[1:], jnp.float32))


def encode(values, peak, message, blocks):
    half = message.shape[2]
    largest = jnp.max(peak, axis=1, keepdims=True)
    largest = jnp.broadcast_to(largest, (peak.shape[0], half))
    level = jnp.ceil(jnp.log2(jnp.maximum(largest, TINY)) * STEPS)
    scale = LEVELS * jnp.exp2(level * (-1.0 / STEPS))
    message[2 * blocks] = level.astype(jnp.int32).astype(jnp.int16)

    def body(j, carry):
        for h in range(2):
            scaled = jnp.round(values[j, :, h * half : (h + 1) * half] * scale)
            message[2 * j + h] = scaled.astype(jnp.int32).astype(jnp.int16)
        return carry

    lax.fori_loop(0, blocks, body, 0)


def unit(message, blocks):
    level = message[2 * blocks].astype(jnp.int32).astype(jnp.float32)
    return jnp.exp2(level * (1.0 / STEPS)) * (1.0 / LEVELS)


def decoded(message, j, h, scale):
    return message[2 * j + h].astype(jnp.int32).astype(jnp.float32) * scale


def kernel(
    lines, row_blocks, blocks, chunks, unroll,
    cols_ref, rows_ref, mask_ref, table_ref, probes_ref, active_ref, tiles_hbm,
    out_ref,
    tiles, gathered, forward, forward_in, weighted, terms, spare, own,
    y_out, y_in, z_out, z_in,
    tile_sem, up_sem, down_sem, over_sem, gather_sem,
    swap_send, swap_recv, y_send, y_recv, z_send, z_recv,
):
    slots, ts = tiles.shape[0], tiles.shape[1]
    probes = gathered.shape[1]
    half = ts // 2
    me = lax.axis_index("row")
    z, y = me // 2, me % 2
    side = lax.axis_index("col")
    above = jnp.minimum(z + 1, lines - 1) * 2 + y
    below = jnp.maximum(z - 1, 0) * 2 + y
    over = z * 2 + 1 - y
    has_above = z < lines - 1
    has_below = z > 0

    per_chunk = slots // chunks

    def tile_copy(i):
        part = pl.ds(i * per_chunk, per_chunk)
        return pltpu.make_async_copy(tiles_hbm.at[part], tiles.at[part], tile_sem.at[i])

    for i in range(chunks):
        tile_copy(i).start()

    barrier = pltpu.get_barrier_semaphore()
    pl.semaphore_signal(barrier, inc=1, device_id={"row": over}, device_id_type=MESH)
    pl.semaphore_signal(barrier, inc=1, device_id={"col": 1 - side}, device_id_type=MESH)

    @pl.when(has_above)
    def _():
        pl.semaphore_signal(barrier, inc=1, device_id={"row": above}, device_id_type=MESH)

    @pl.when(has_below)
    def _():
        pl.semaphore_signal(barrier, inc=1, device_id={"row": below}, device_id_type=MESH)

    for j in range(blocks):
        gathered[me * blocks + j] = probes_ref[:, j * ts : (j + 1) * ts]
    terms[slots] = jnp.zeros((probes, ts), jnp.float32)

    pl.semaphore_wait(barrier, 2 + jnp.where(has_above, 1, 0) + jnp.where(has_below, 1, 0))

    def shard_copy(r, sem, k, target):
        part = pl.ds(r * blocks, blocks)
        return pltpu.make_async_remote_copy(
            src_ref=gathered.at[part], dst_ref=gathered.at[part],
            send_sem=sem.at[k], recv_sem=gather_sem.at[r],
            device_id={"row": target}, device_id_type=MESH,
        )

    def pass_on(line, go_up, go_down):
        r = line * 2 + y

        @pl.when(go_up)
        def _():
            shard_copy(r, up_sem, line, above).start()

        @pl.when(go_down)
        def _():
            shard_copy(r, down_sem, line, below).start()

        shard_copy(r, over_sem, line, over).start()

    pass_on(z, has_above, has_below)

    def gather_step(k, carry):
        @pl.when(z >= k)
        def _():
            shard_copy((z - k) * 2 + y, up_sem, z - k, over).wait_recv()
            pass_on(z - k, has_above, False)

        @pl.when(z + k < lines)
        def _():
            shard_copy((z + k) * 2 + y, down_sem, z + k, over).wait_recv()
            pass_on(z + k, False, has_below)

        return carry

    lax.fori_loop(1, lines, gather_step, 0)

    def gather_end(line, carry):
        shard_copy(line * 2 + 1 - y, over_sem, line, over).wait_recv()
        shard_copy(line * 2 + y, over_sem, line, over).wait_send()

        @pl.when(has_above & (line <= z))
        def _():
            shard_copy(line * 2 + y, up_sem, line, above).wait_send()

        @pl.when(has_below & (line >= z))
        def _():
            shard_copy(line * 2 + y, down_sem, line, below).wait_send()

        return carry

    lax.fori_loop(0, lines, gather_end, 0)
    for i in range(chunks):
        tile_copy(i).wait()

    forward[...] = jnp.zeros_like(forward)

    def forward_step(i, carry):
        total = None
        for u in range(unroll):
            s = i * unroll + u
            x = gathered[cols_ref[s]]
            spread = jnp.concatenate(
                [
                    x * jnp.full(x.shape, mask_ref[s * row_blocks + b], jnp.float32).astype(x.dtype)
                    for b in range(row_blocks)
                ],
                axis=0,
            )
            product = lax.dot_general(
                spread, tiles[s], (((1,), (1,)), ((), ())), preferred_element_type=jnp.float32
            )
            total = product if total is None else total + product
        forward[...] += total
        return carry

    lax.fori_loop(0, slots // unroll, forward_step, 0)

    swap = pltpu.make_async_remote_copy(
        src_ref=forward, dst_ref=forward_in, send_sem=swap_send, recv_sem=swap_recv,
        device_id={"col": 1 - side}, device_id_type=MESH,
    )
    swap.start()
    swap.wait()
    for b in range(row_blocks):
        part = slice(b * probes, (b + 1) * probes)
        row_sum = forward[part] + forward_in[part]
        weighted[b] = (row_sum * active_ref[b]).astype(weighted.dtype)

    def back_step(i, carry):
        for u in range(unroll):
            s = i * unroll + u
            terms[s] = jnp.dot(
                weighted[rows_ref[s]], tiles[s], preferred_element_type=jnp.float32
            )
        return carry

    lax.fori_loop(0, slots // unroll, back_step, 0)

    def y_copy(line):
        return pltpu.make_async_remote_copy(
            src_ref=y_out.at[line], dst_ref=y_in.at[line],
            send_sem=y_send.at[line], recv_sem=y_recv.at[line],
            device_id={"row": over}, device_id_type=MESH,
        )

    def y_start(line):
        peak = combine(table_ref, terms, line * 2 + 1 - y, blocks, row_blocks, spare)
        encode(spare, peak, y_out.at[line], blocks)
        y_copy(line).start()

    def y_step(i, carry):
        k = lines - 1 - i

        @pl.when(z >= k)
        def _():
            y_start(z - k)

        @pl.when(z + k < lines)
        def _():
            y_start(z + k)

        return carry

    lax.fori_loop(0, lines - 1, y_step, 0)
    y_start(z)

    def own_step(line, carry):
        combine(table_ref, terms, line * 2 + y, blocks, row_blocks, own.at[line])
        return carry

    lax.fori_loop(0, lines, own_step, 0)

    def z_copy(line, slot, target):
        return pltpu.make_async_remote_copy(
            src_ref=z_out.at[line], dst_ref=z_in.at[slot],
            send_sem=z_send.at[line], recv_sem=z_recv.at[slot],
            device_id={"row": target}, device_id_type=MESH,
        )

    def add_in(total, message):
        scale = unit(message, blocks)

        def body(j, peak):
            sums = []
            for h in range(2):
                lanes = slice(h * half, (h + 1) * half)
                value = total[j, :, lanes] + decoded(message, j, h, scale)
                total[j, :, lanes] = value
                sums.append(jnp.abs(value))
            return jnp.maximum(peak, jnp.maximum(*sums))

        return lax.fori_loop(0, blocks, body, jnp.zeros((probes, half), jnp.float32))

    def z_start(line, upstream, slot, target):
        y_copy(line).wait_recv()
        peak = add_in(own.at[line], y_in.at[line])
        spare_peak[...] = peak

        @pl.when(upstream)
        def _():
            z_copy(line, line, target).wait_recv()
            spare_peak[...] = add_in(own.at[line], z_in.at[line])

        encode(own.at[line], spare_peak[...], z_out.at[line], blocks)
        z_copy(line, slot, target).start()

    spare_peak = spare.at[0, :, pl.ds(0, half)]

    def z_step(i, carry):
        k = lines - 1 - i

        @pl.when(z >= k)
        def _():
            z_start(z - k, has_above, jnp.where(k == 1, lines, z - k), below)

        @pl.when(z + k < lines)
        def _():
            z_start(z + k, has_below, z + k, above)

        return carry

    lax.fori_loop(0, lines - 1, z_step, 0)

    total = own.at[z]
    y_copy(z).wait_recv()
    add_in(total, y_in.at[z])

    @pl.when(has_below)
    def _():
        z_copy(z, z, below).wait_recv()
        add_in(total, z_in.at[z])

    @pl.when(has_above)
    def _():
        z_copy(z, lines, above).wait_recv()
        add_in(total, z_in.at[lines])

    for j in range(blocks):
        out_ref[:, j * ts : (j + 1) * ts] = total[j]

    def z_end(line, carry):
        y_copy(line).wait_send()

        @pl.when(line != z)
        def _():
            z_copy(line, line, over).wait_send()

        return carry

    lax.fori_loop(0, lines, z_end, 0)


def on_device(row_devices, probes, tile_data, tile_rows, tile_cols, tile_count, active):
    tiles = tile_data[0, 0]
    slot_rows = tile_rows[0, 0]
    slot_cols = tile_cols[0, 0]
    live_count = tile_count[0, 0, 0]
    slots, ts = tiles.shape[0], tiles.shape[1]
    probe_count, owned = probes.shape[1], probes.shape[2]
    blocks = owned // ts
    col_blocks = row_devices * blocks
    row_blocks = active.shape[0] // ts
    lines = row_devices // 2
    chunks = 8 if slots % 8 == 0 else 1
    unroll = 4 if slots % 4 == 0 else 1

    index = jnp.arange(slots, dtype=jnp.int32)
    live = index < live_count
    mask = (slot_rows[:, None] == jnp.arange(row_blocks)[None, :]) & live[:, None]
    mask = mask.astype(jnp.float32).reshape(-1)
    pair = jnp.where(live, slot_cols * row_blocks + slot_rows, -1)
    place = jnp.arange(col_blocks * row_blocks, dtype=jnp.int32)
    table = jnp.min(jnp.where(place[:, None] == pair[None, :], index[None, :], slots), axis=1)

    smem = pl.BlockSpec(memory_space=pltpu.SMEM)
    vmem = pl.BlockSpec(memory_space=pltpu.VMEM)
    f32, bf16, dma = jnp.float32, jnp.bfloat16, pltpu.SemaphoreType.DMA
    message = (2 * blocks + 1, probe_count, ts // 2)
    back = pl.pallas_call(
        functools.partial(kernel, lines, row_blocks, blocks, chunks, unroll),
        out_shape=jax.ShapeDtypeStruct((probe_count, owned), f32),
        in_specs=[smem, smem, smem, smem, vmem, vmem, pl.BlockSpec(memory_space=pl.ANY)],
        out_specs=vmem,
        scratch_shapes=[
            pltpu.VMEM(tiles.shape, bf16),
            pltpu.VMEM((col_blocks, probe_count, ts), bf16),
            pltpu.VMEM((row_blocks * probe_count, ts), f32),
            pltpu.VMEM((row_blocks * probe_count, ts), f32),
            pltpu.VMEM((row_blocks, probe_count, ts), bf16),
            pltpu.VMEM((slots + 1, probe_count, ts), f32),
            pltpu.VMEM((blocks, probe_count, ts), f32),
            pltpu.VMEM((lines, blocks, probe_count, ts), f32),
            pltpu.VMEM((lines,) + message, jnp.int16),
            pltpu.VMEM((lines,) + message, jnp.int16),
            pltpu.VMEM((lines,) + message, jnp.int16),
            pltpu.VMEM((lines + 1,) + message, jnp.int16),
            dma((chunks,)), dma((lines,)), dma((lines,)), dma((lines,)), dma((row_devices,)),
            dma, dma, dma((lines,)), dma((lines,)), dma((lines,)), dma((lines + 1,)),
        ],
        compiler_params=pltpu.CompilerParams(
            collective_id=0, has_side_effects=True, vmem_limit_bytes=56 * 1024 * 1024
        ),
        cost_estimate=pl.CostEstimate(
            flops=2 * slots * ts * ts * probe_count * (row_blocks + 1),
            bytes_accessed=2 * tiles.size, transcendentals=0,
        ),
    )(
        slot_cols, slot_rows, mask, table,
        probes[0], active.astype(f32).reshape(row_blocks, 1, ts), tiles,
    )
    return (probes[0].astype(f32) + back)[None]


def solution(mesh):
    placed = (
        P(("groups", "col"), None, "row"),
        P(("groups", "row"), "col", None, None, None),
        P(("groups", "row"), "col", None),
        P(("groups", "row"), "col", None),
        P(("groups", "row"), "col", None),
        P(("groups", "row")),
    )
    return jax.shard_map(
        functools.partial(on_device, mesh.shape["row"]),
        mesh=mesh,
        in_specs=placed,
        out_specs=P(("groups", "col"), None, "row"),
        check_vma=False,
    )
```

```python
import functools

import jax
import jax.numpy as jnp
from jax import lax
from jax.experimental import pallas as pl
from jax.experimental.pallas import tpu as pltpu
from jax.sharding import PartitionSpec as P

MESH = pl.DeviceIdType.MESH
LEVELS = 32000.0
STEPS = 256.0
TINY = 1e-30


def over_blocks(blocks, body, start):
    step = 4 if blocks % 4 == 0 else 1

    def several(i, carry):
        for u in range(step):
            carry = body(i * step + u, carry)
        return carry

    return lax.fori_loop(0, blocks // step, several, start)


def combine(table_ref, terms, dest, blocks, row_blocks, out):
    def body(j, peak):
        col = dest * blocks + j
        total = terms[table_ref[0, col]]
        for k in range(1, row_blocks):
            total = total + terms[table_ref[k, col]]
        out[j] = total
        return jnp.maximum(peak, jnp.abs(total))

    return over_blocks(blocks, body, jnp.zeros(out.shape[1:], jnp.float32))


def encode(values, peak, message, blocks):
    half = message.shape[2]
    largest = jnp.max(peak, axis=1, keepdims=True)
    largest = jnp.broadcast_to(largest, (peak.shape[0], half))
    level = jnp.ceil(jnp.log2(jnp.maximum(largest, TINY)) * STEPS)
    scale = LEVELS * jnp.exp2(level * (-1.0 / STEPS))
    message[2 * blocks] = level.astype(jnp.int32).astype(jnp.int16)

    def body(j, carry):
        for h in range(2):
            scaled = jnp.round(values[j, :, h * half : (h + 1) * half] * scale)
            message[2 * j + h] = scaled.astype(jnp.int32).astype(jnp.int16)
        return carry

    over_blocks(blocks, body, 0)


def unit(message, blocks):
    level = message[2 * blocks].astype(jnp.int32).astype(jnp.float32)
    return jnp.exp2(level * (1.0 / STEPS)) * (1.0 / LEVELS)


def decoded(message, j, h, scale):
    return message[2 * j + h].astype(jnp.int32).astype(jnp.float32) * scale


def kernel(
    lines, row_blocks, blocks, chunks, unroll, parts,
    cols_ref, rows_ref, count_ref, probes_ref, active_ref, tiles_hbm,
    out_ref,
    tiles, turned, gathered_first, gathered_second, forward, forward_in, weighted, terms, spare, own,
    y_out, y_in, z_out, z_in, table_vmem, table_ref,
    tile_sem, table_sem, up_sem, down_sem, over_sem, gather_sem,
    swap_send, swap_recv, y_send, y_recv, z_send, z_recv,
):
    slots, ts = tiles.shape[0], tiles.shape[1]
    gathered = (gathered_first, gathered_second)
    probes = gathered_first.shape[1]
    half = ts // 2
    me = lax.axis_index("row")
    z, y = me // 2, me % 2
    side = lax.axis_index("col")
    above = jnp.minimum(z + 1, lines - 1) * 2 + y
    below = jnp.maximum(z - 1, 0) * 2 + y
    over = z * 2 + 1 - y
    has_above = z < lines - 1
    has_below = z > 0

    per_chunk = slots // chunks

    def tile_copy(i):
        part = pl.ds(i * per_chunk, per_chunk)
        return pltpu.make_async_copy(tiles_hbm.at[part], tiles.at[part], tile_sem.at[i])

    barrier = pltpu.get_barrier_semaphore()
    pl.semaphore_signal(barrier, inc=1, device_id={"row": over}, device_id_type=MESH)
    pl.semaphore_signal(barrier, inc=1, device_id={"col": 1 - side}, device_id_type=MESH)

    @pl.when(has_above)
    def _():
        pl.semaphore_signal(barrier, inc=1, device_id={"row": above}, device_id_type=MESH)

    @pl.when(has_below)
    def _():
        pl.semaphore_signal(barrier, inc=1, device_id={"row": below}, device_id_type=MESH)

    for i in range(chunks):
        tile_copy(i).start()

    for h in range(parts):
        for j in range(blocks):
            gathered[h][me * blocks + j] = probes_ref[
                h * probes : (h + 1) * probes, j * ts : (j + 1) * ts
            ]

    pl.semaphore_wait(barrier, 2 + jnp.where(has_above, 1, 0) + jnp.where(has_below, 1, 0))

    def shard_copy(h, r, sem, k, target):
        part = pl.ds(r * blocks, blocks)
        return pltpu.make_async_remote_copy(
            src_ref=gathered[h].at[part], dst_ref=gathered[h].at[part],
            send_sem=sem.at[h, k], recv_sem=gather_sem.at[h, r],
            device_id={"row": target}, device_id_type=MESH,
        )

    def pass_on(h, line, go_up, go_down):
        r = line * 2 + y

        @pl.when(go_up)
        def _():
            shard_copy(h, r, up_sem, line, above).start()

        @pl.when(go_down)
        def _():
            shard_copy(h, r, down_sem, line, below).start()

        shard_copy(h, r, over_sem, line, over).start()

    def gather_steps(h, first, last):
        def step(k, carry):
            @pl.when(z >= k)
            def _():
                shard_copy(h, (z - k) * 2 + y, up_sem, z - k, over).wait_recv()
                pass_on(h, z - k, has_above, False)

            @pl.when(z + k < lines)
            def _():
                shard_copy(h, (z + k) * 2 + y, down_sem, z + k, over).wait_recv()
                pass_on(h, z + k, False, has_below)

            return carry

        lax.fori_loop(first, last, step, 0)

    def gather_end(h):
        def step(line, carry):
            shard_copy(h, line * 2 + 1 - y, over_sem, line, over).wait_recv()
            shard_copy(h, line * 2 + y, over_sem, line, over).wait_send()

            @pl.when(has_above & (line <= z))
            def _():
                shard_copy(h, line * 2 + y, up_sem, line, above).wait_send()

            @pl.when(has_below & (line >= z))
            def _():
                shard_copy(h, line * 2 + y, down_sem, line, below).wait_send()

            return carry

        lax.fori_loop(0, lines, step, 0)

    def forward_steps(h, first, last):
        def step(i, carry):
            total = None
            for u in range(unroll):
                s = i * unroll + u
                x = gathered[h][cols_ref[0, 0, s]]
                row = jnp.where(s < count_ref[0, 0, 0], rows_ref[0, 0, s], -1)
                spread = jnp.concatenate(
                    [
                        x * jnp.full(x.shape, jnp.where(row == b, 1.0, 0.0), jnp.float32).astype(x.dtype)
                        for b in range(row_blocks)
                    ],
                    axis=0,
                )
                product = jnp.dot(spread, turned[s], preferred_element_type=jnp.float32)
                total = product if total is None else total + product
            forward[h] += total
            return carry

        lax.fori_loop(first, last, step, 0)

    def swap(h):
        return pltpu.make_async_remote_copy(
            src_ref=forward.at[h], dst_ref=forward_in.at[h],
            send_sem=swap_send.at[h], recv_sem=swap_recv.at[h],
            device_id={"col": 1 - side}, device_id_type=MESH,
        )

    def weigh(h):
        for b in range(row_blocks):
            part = slice(b * probes, (b + 1) * probes)
            row_sum = forward[h, part] + forward_in[h, part]
            mask = jnp.concatenate(
                [active_ref[2 * b + i : 2 * b + i + 1, :] for i in range(2)], axis=1
            ).astype(jnp.float32)
            weighted[h, b] = (row_sum * mask).astype(weighted.dtype)

    def back_steps(h, first, last):
        def step(i, carry):
            for u in range(unroll):
                s = i * unroll + u
                terms[h, s] = jnp.dot(
                    weighted[h, rows_ref[0, 0, s]], tiles[s], preferred_element_type=jnp.float32
                )
            return carry

        lax.fori_loop(first, last, step, 0)

    def y_copy(h, line):
        return pltpu.make_async_remote_copy(
            src_ref=y_out.at[h, line], dst_ref=y_in.at[h, line],
            send_sem=y_send.at[h, line], recv_sem=y_recv.at[h, line],
            device_id={"row": over}, device_id_type=MESH,
        )

    def y_start(h, line):
        peak = combine(table_ref, terms.at[h], line * 2 + 1 - y, blocks, row_blocks, spare)
        encode(spare, peak, y_out.at[h, line], blocks)
        y_copy(h, line).start()

    def y_all(h):
        def step(i, carry):
            k = lines - 1 - i

            @pl.when(z >= k)
            def _():
                y_start(h, z - k)

            @pl.when(z + k < lines)
            def _():
                y_start(h, z + k)

            return carry

        lax.fori_loop(0, lines - 1, step, 0)
        y_start(h, z)

        def own_step(line, carry):
            combine(table_ref, terms.at[h], line * 2 + y, blocks, row_blocks, own.at[h, line])
            return carry

        lax.fori_loop(0, lines, own_step, 0)

    def z_copy(h, line, slot, target):
        return pltpu.make_async_remote_copy(
            src_ref=z_out.at[h, line], dst_ref=z_in.at[h, slot],
            send_sem=z_send.at[h, line], recv_sem=z_recv.at[h, slot],
            device_id={"row": target}, device_id_type=MESH,
        )

    def add_in(total, message):
        scale = unit(message, blocks)

        def body(j, peak):
            sums = []
            for i in range(2):
                lanes = slice(i * half, (i + 1) * half)
                value = total[j, :, lanes] + decoded(message, j, i, scale)
                total[j, :, lanes] = value
                sums.append(jnp.abs(value))
            return jnp.maximum(peak, jnp.maximum(*sums))

        return over_blocks(blocks, body, jnp.zeros((probes, half), jnp.float32))

    peak_ref = spare.at[0, :, pl.ds(0, half)]

    def z_start(h, line, upstream, slot, target):
        y_copy(h, line).wait_recv()
        peak_ref[...] = add_in(own.at[h, line], y_in.at[h, line])

        @pl.when(upstream)
        def _():
            z_copy(h, line, line, target).wait_recv()
            peak_ref[...] = add_in(own.at[h, line], z_in.at[h, line])

        encode(own.at[h, line], peak_ref[...], z_out.at[h, line], blocks)
        z_copy(h, line, slot, target).start()

    def z_steps(h, first, last):
        def step(i, carry):
            k = lines - i

            @pl.when(z >= k)
            def _():
                z_start(h, z - k, has_above, jnp.where(k == 1, lines, z - k), below)

            @pl.when(z + k < lines)
            def _():
                z_start(h, z + k, has_below, z + k, above)

            return carry

        lax.fori_loop(first, last, step, 0)

    def finish(h):
        total = own.at[h, z]
        y_copy(h, z).wait_recv()
        add_in(total, y_in.at[h, z])

        @pl.when(has_below)
        def _():
            z_copy(h, z, z, below).wait_recv()
            add_in(total, z_in.at[h, z])

        @pl.when(has_above)
        def _():
            z_copy(h, z, lines, above).wait_recv()
            add_in(total, z_in.at[h, lines])

        for j in range(blocks):
            out_ref[h * probes : (h + 1) * probes, j * ts : (j + 1) * ts] = total[j]

    def z_end(h):
        def step(line, carry):
            y_copy(h, line).wait_send()

            @pl.when(line != z)
            def _():
                z_copy(h, line, line, over).wait_send()

            return carry

        lax.fori_loop(0, lines, step, 0)

    groups = slots // unroll
    middle = groups // 2
    cuts = [1 + (lines - 1) * i // 3 for i in range(4)]

    def compute(h, beside):
        forward_steps(h, 0, middle)
        beside(cuts[0], cuts[1])
        forward_steps(h, middle, groups)
        swap(h).start()
        beside(cuts[1], cuts[2])
        swap(h).wait()
        weigh(h)
        back_steps(h, 0, middle)
        beside(cuts[2], cuts[3])
        back_steps(h, middle, groups)

    pass_on(0, z, has_above, has_below)

    shape = table_vmem.shape
    place = lax.broadcasted_iota(jnp.int32, shape, 1) * row_blocks + lax.broadcasted_iota(jnp.int32, shape, 0)

    def table_step(s, table):
        pair = jnp.where(s < count_ref[0, 0, 0], cols_ref[0, 0, s] * row_blocks + rows_ref[0, 0, s], -1)
        return jnp.where(place == pair, s, table)

    table_vmem[...] = lax.fori_loop(0, slots, table_step, jnp.full(shape, slots, jnp.int32))
    table_copy = pltpu.make_async_copy(table_vmem, table_ref, table_sem)
    table_copy.start()
    for h in range(parts):
        terms[h, slots] = jnp.zeros((probes, ts), jnp.float32)
        forward[h] = jnp.zeros(forward.shape[1:], jnp.float32)

    turns = [1 + min(lines - 1, (lines - 1) * i * 4 // (3 * chunks)) for i in range(chunks + 1)]

    for i in range(chunks):
        tile_copy(i).wait()

        def turn_step(n, carry):
            for u in range(2):
                s = i * per_chunk + n * 2 + u
                turned[s] = tiles[s].T
            return carry

        lax.fori_loop(0, per_chunk // 2, turn_step, 0)
        gather_steps(0, turns[i], turns[i + 1])
        if turns[i] < turns[i + 1] == lines:
            pass_on(1, z, has_above, has_below)
    table_copy.wait()
    gather_end(0)
    for h in range(parts):
        compute(h, functools.partial(gather_steps, 1) if h == 0 else functools.partial(z_steps, 0))
        y_all(h)
        if h == 0:
            gather_end(1)
    finish(0)
    z_steps(1, 1, lines)
    finish(1)
    z_end(0)
    z_end(1)


def on_device(row_devices, probes, tile_data, tile_rows, tile_cols, tile_count, active):
    tiles = tile_data[0, 0]
    slots, ts = tiles.shape[0], tiles.shape[1]
    probe_count, owned = probes.shape[1], probes.shape[2]
    blocks = owned // ts
    col_blocks = row_devices * blocks
    row_blocks = active.shape[0] // ts
    lines = row_devices // 2
    chunks = 8 if slots % 16 == 0 else 1
    unroll = 16 if slots % 16 == 0 else 1
    parts = 2
    share = probe_count // parts

    smem = pl.BlockSpec(memory_space=pltpu.SMEM)
    vmem = pl.BlockSpec(memory_space=pltpu.VMEM)
    f32, bf16, dma = jnp.float32, jnp.bfloat16, pltpu.SemaphoreType.DMA
    message = (2 * blocks + 1, share, ts // 2)
    back = pl.pallas_call(
        functools.partial(kernel, lines, row_blocks, blocks, chunks, unroll, parts),
        out_shape=jax.ShapeDtypeStruct((probe_count, owned), f32),
        in_specs=[smem, smem, smem, vmem, vmem, pl.BlockSpec(memory_space=pl.ANY)],
        out_specs=vmem,
        scratch_shapes=[
            pltpu.VMEM(tiles.shape, bf16),
            pltpu.VMEM(tiles.shape, bf16),
            pltpu.VMEM((col_blocks, share, ts), bf16),
            pltpu.VMEM((col_blocks, share, ts), bf16),
            pltpu.VMEM((parts, row_blocks * share, ts), f32),
            pltpu.VMEM((parts, row_blocks * share, ts), f32),
            pltpu.VMEM((parts, row_blocks, share, ts), bf16),
            pltpu.VMEM((parts, slots + 1, share, ts), f32),
            pltpu.VMEM((blocks, share, ts), f32),
            pltpu.VMEM((parts, lines, blocks, share, ts), f32),
            pltpu.VMEM((parts, lines) + message, jnp.int16),
            pltpu.VMEM((parts, lines) + message, jnp.int16),
            pltpu.VMEM((parts, lines) + message, jnp.int16),
            pltpu.VMEM((parts, lines + 1) + message, jnp.int16),
            pltpu.VMEM((row_blocks, col_blocks), jnp.int32),
            pltpu.SMEM((row_blocks, col_blocks), jnp.int32),
            dma((chunks,)), dma,
            dma((parts, lines)), dma((parts, lines)), dma((parts, lines)), dma((parts, row_devices)),
            dma((parts,)), dma((parts,)),
            dma((parts, lines)), dma((parts, lines)), dma((parts, lines)), dma((parts, lines + 1)),
        ],
        compiler_params=pltpu.CompilerParams(
            collective_id=0, has_side_effects=True, vmem_limit_bytes=56 * 1024 * 1024
        ),
        cost_estimate=pl.CostEstimate(
            flops=2 * slots * ts * ts * probe_count * (row_blocks + 1),
            bytes_accessed=2 * tiles.size, transcendentals=0,
        ),
    )(
        tile_cols, tile_rows, tile_count,
        probes[0], active.reshape(row_blocks * 2, ts // 2), tiles,
    )
    return (probes[0].astype(f32) + back)[None]


def solution(mesh):
    placed = (
        P(("groups", "col"), None, "row"),
        P(("groups", "row"), "col", None, None, None),
        P(("groups", "row"), "col", None),
        P(("groups", "row"), "col", None),
        P(("groups", "row"), "col", None),
        P(("groups", "row")),
    )
    return jax.shard_map(
        functools.partial(on_device, mesh.shape["row"]),
        mesh=mesh,
        in_specs=placed,
        out_specs=P(("groups", "col"), None, "row"),
        check_vma=False,
    )
```

```python
import functools

import jax
import jax.numpy as jnp
from jax import lax
from jax.experimental import pallas as pl
from jax.experimental.pallas import tpu as pltpu
from jax.sharding import PartitionSpec as P

MESH = pl.DeviceIdType.MESH
LEVELS = 32000.0
STEPS = 256.0
TINY = 1e-30


def over_blocks(blocks, body, start):
    step = 4 if blocks % 4 == 0 else 1

    def several(i, carry):
        for u in range(step):
            carry = body(i * step + u, carry)
        return carry

    return lax.fori_loop(0, blocks // step, several, start)


def combine(table_ref, terms, dest, blocks, row_blocks, out):
    def body(j, peak):
        col = dest * blocks + j
        total = terms[table_ref[0, col]]
        for k in range(1, row_blocks):
            total = total + terms[table_ref[k, col]]
        out[j] = total
        return jnp.maximum(peak, jnp.abs(total))

    return over_blocks(blocks, body, jnp.zeros(out.shape[1:], jnp.float32))


def encode(values, peak, message, blocks):
    half = message.shape[2]
    largest = jnp.max(peak, axis=1, keepdims=True)
    largest = jnp.broadcast_to(largest, (peak.shape[0], half))
    level = jnp.ceil(jnp.log2(jnp.maximum(largest, TINY)) * STEPS)
    scale = LEVELS * jnp.exp2(level * (-1.0 / STEPS))
    message[2 * blocks] = level.astype(jnp.int32).astype(jnp.int16)

    def body(j, carry):
        for h in range(2):
            scaled = jnp.round(values[j, :, h * half : (h + 1) * half] * scale)
            message[2 * j + h] = scaled.astype(jnp.int32).astype(jnp.int16)
        return carry

    over_blocks(blocks, body, 0)


def unit(message, blocks):
    level = message[2 * blocks].astype(jnp.int32).astype(jnp.float32)
    return jnp.exp2(level * (1.0 / STEPS)) * (1.0 / LEVELS)


def decoded(message, j, h, scale):
    return message[2 * j + h].astype(jnp.int32).astype(jnp.float32) * scale


def kernel(
    lines, row_blocks, blocks, chunks, unroll, parts,
    cols_ref, rows_ref, count_ref, probes_ref, active_ref, tiles_hbm,
    out_ref,
    tiles, turned, gathered_first, gathered_second, forward, forward_in, weighted, terms, spare, own,
    y_out, y_in, z_out, z_in, table_vmem, table_ref,
    tile_sem, table_sem, up_sem, down_sem, over_sem, gather_sem,
    swap_send, swap_recv, y_send, y_recv, z_send, z_recv,
):
    slots, ts = tiles.shape[0], tiles.shape[1]
    gathered = (gathered_first, gathered_second)
    probes = gathered_first.shape[1]
    half = ts // 2
    me = lax.axis_index("row")
    z, y = me // 2, me % 2
    side = lax.axis_index("col")
    above = jnp.minimum(z + 1, lines - 1) * 2 + y
    below = jnp.maximum(z - 1, 0) * 2 + y
    over = z * 2 + 1 - y
    has_above = z < lines - 1
    has_below = z > 0

    per_chunk = slots // chunks

    def tile_copy(i):
        part = pl.ds(i * per_chunk, per_chunk)
        return pltpu.make_async_copy(tiles_hbm.at[part], tiles.at[part], tile_sem.at[i])

    barrier = pltpu.get_barrier_semaphore()
    pl.semaphore_signal(barrier, inc=1, device_id={"row": over}, device_id_type=MESH)
    pl.semaphore_signal(barrier, inc=1, device_id={"col": 1 - side}, device_id_type=MESH)

    @pl.when(has_above)
    def _():
        pl.semaphore_signal(barrier, inc=1, device_id={"row": above}, device_id_type=MESH)

    @pl.when(has_below)
    def _():
        pl.semaphore_signal(barrier, inc=1, device_id={"row": below}, device_id_type=MESH)

    for i in range(chunks):
        tile_copy(i).start()

    for h in range(parts):
        for j in range(blocks):
            gathered[h][me * blocks + j] = probes_ref[
                h * probes : (h + 1) * probes, j * ts : (j + 1) * ts
            ]

    pl.semaphore_wait(barrier, 2 + jnp.where(has_above, 1, 0) + jnp.where(has_below, 1, 0))

    def shard_copy(h, r, sem, k, target):
        part = pl.ds(r * blocks, blocks)
        return pltpu.make_async_remote_copy(
            src_ref=gathered[h].at[part], dst_ref=gathered[h].at[part],
            send_sem=sem.at[h, k], recv_sem=gather_sem.at[h, r],
            device_id={"row": target}, device_id_type=MESH,
        )

    def pass_on(h, line, go_up, go_down):
        r = line * 2 + y

        @pl.when(go_up)
        def _():
            shard_copy(h, r, up_sem, line, above).start()

        @pl.when(go_down)
        def _():
            shard_copy(h, r, down_sem, line, below).start()

        shard_copy(h, r, over_sem, line, over).start()

    def gather_steps(h, first, last):
        def step(k, carry):
            @pl.when(z >= k)
            def _():
                shard_copy(h, (z - k) * 2 + y, up_sem, z - k, over).wait_recv()
                pass_on(h, z - k, has_above, False)

            @pl.when(z + k < lines)
            def _():
                shard_copy(h, (z + k) * 2 + y, down_sem, z + k, over).wait_recv()
                pass_on(h, z + k, False, has_below)

            return carry

        lax.fori_loop(first, last, step, 0)

    def gather_end(h):
        def step(line, carry):
            shard_copy(h, line * 2 + 1 - y, over_sem, line, over).wait_recv()
            shard_copy(h, line * 2 + y, over_sem, line, over).wait_send()

            @pl.when(has_above & (line <= z))
            def _():
                shard_copy(h, line * 2 + y, up_sem, line, above).wait_send()

            @pl.when(has_below & (line >= z))
            def _():
                shard_copy(h, line * 2 + y, down_sem, line, below).wait_send()

            return carry

        lax.fori_loop(0, lines, step, 0)

    def forward_steps(h, first, last):
        def step(i, carry):
            total = None
            for u in range(unroll):
                s = i * unroll + u
                x = gathered[h][cols_ref[0, 0, s]]
                row = jnp.where(s < count_ref[0, 0, 0], rows_ref[0, 0, s], -1)
                spread = jnp.concatenate(
                    [
                        x * jnp.full(x.shape, jnp.where(row == b, 1.0, 0.0), jnp.float32).astype(x.dtype)
                        for b in range(row_blocks)
                    ],
                    axis=0,
                )
                product = jnp.dot(spread, turned[s], preferred_element_type=jnp.float32)
                total = product if total is None else total + product
            forward[h] += total
            return carry

        lax.fori_loop(first, last, step, 0)

    def swap(h):
        return pltpu.make_async_remote_copy(
            src_ref=forward.at[h], dst_ref=forward_in.at[h],
            send_sem=swap_send.at[h], recv_sem=swap_recv.at[h],
            device_id={"col": 1 - side}, device_id_type=MESH,
        )

    def weigh(h):
        for b in range(row_blocks):
            part = slice(b * probes, (b + 1) * probes)
            row_sum = forward[h, part] + forward_in[h, part]
            mask = jnp.concatenate(
                [active_ref[2 * b + i : 2 * b + i + 1, :] for i in range(2)], axis=1
            ).astype(jnp.float32)
            weighted[h, b] = (row_sum * mask).astype(weighted.dtype)

    def back_steps(h, first, last):
        def step(i, carry):
            for u in range(unroll):
                s = i * unroll + u
                terms[h, s] = jnp.dot(
                    weighted[h, rows_ref[0, 0, s]], tiles[s], preferred_element_type=jnp.float32
                )
            return carry

        lax.fori_loop(first, last, step, 0)

    def y_copy(h, line):
        return pltpu.make_async_remote_copy(
            src_ref=y_out.at[h, line], dst_ref=y_in.at[h, line],
            send_sem=y_send.at[h, line], recv_sem=y_recv.at[h, line],
            device_id={"row": over}, device_id_type=MESH,
        )

    def y_start(h, line):
        peak = combine(table_ref, terms.at[h], line * 2 + 1 - y, blocks, row_blocks, spare)
        encode(spare, peak, y_out.at[h, line], blocks)
        y_copy(h, line).start()

    def y_all(h):
        def step(i, carry):
            k = lines - 1 - i

            @pl.when(z >= k)
            def _():
                y_start(h, z - k)

            @pl.when(z + k < lines)
            def _():
                y_start(h, z + k)

            return carry

        lax.fori_loop(0, lines - 1, step, 0)
        y_start(h, z)

        def own_step(line, carry):
            combine(table_ref, terms.at[h], line * 2 + y, blocks, row_blocks, own.at[h, line])
            return carry

        lax.fori_loop(0, lines, own_step, 0)

    def z_copy(h, line, slot, target):
        return pltpu.make_async_remote_copy(
            src_ref=z_out.at[h, line], dst_ref=z_in.at[h, slot],
            send_sem=z_send.at[h, line], recv_sem=z_recv.at[h, slot],
            device_id={"row": target}, device_id_type=MESH,
        )

    def add_in(total, message):
        scale = unit(message, blocks)

        def body(j, peak):
            sums = []
            for i in range(2):
                lanes = slice(i * half, (i + 1) * half)
                value = total[j, :, lanes] + decoded(message, j, i, scale)
                total[j, :, lanes] = value
                sums.append(jnp.abs(value))
            return jnp.maximum(peak, jnp.maximum(*sums))

        return over_blocks(blocks, body, jnp.zeros((probes, half), jnp.float32))

    peak_ref = spare.at[0, :, pl.ds(0, half)]

    def z_start(h, line, upstream, slot, target):
        y_copy(h, line).wait_recv()
        peak_ref[...] = add_in(own.at[h, line], y_in.at[h, line])

        @pl.when(upstream)
        def _():
            z_copy(h, line, line, target).wait_recv()
            peak_ref[...] = add_in(own.at[h, line], z_in.at[h, line])

        encode(own.at[h, line], peak_ref[...], z_out.at[h, line], blocks)
        z_copy(h, line, slot, target).start()

    def z_steps(h, first, last):
        def step(i, carry):
            k = lines - i

            @pl.when(z >= k)
            def _():
                z_start(h, z - k, has_above, jnp.where(k == 1, lines, z - k), below)

            @pl.when(z + k < lines)
            def _():
                z_start(h, z + k, has_below, z + k, above)

            return carry

        lax.fori_loop(first, last, step, 0)

    def finish(h):
        total = own.at[h, z]
        y_copy(h, z).wait_recv()
        add_in(total, y_in.at[h, z])

        @pl.when(has_below)
        def _():
            z_copy(h, z, z, below).wait_recv()
            add_in(total, z_in.at[h, z])

        @pl.when(has_above)
        def _():
            z_copy(h, z, lines, above).wait_recv()
            add_in(total, z_in.at[h, lines])

        for j in range(blocks):
            out_ref[h * probes : (h + 1) * probes, j * ts : (j + 1) * ts] = total[j]

    def z_end(h):
        def step(line, carry):
            y_copy(h, line).wait_send()

            @pl.when(line != z)
            def _():
                z_copy(h, line, line, over).wait_send()

            return carry

        lax.fori_loop(0, lines, step, 0)

    groups = slots // unroll
    middle = groups // 2
    cuts = [1 + (lines - 1) * i // 3 for i in range(4)]

    def compute(h, beside):
        forward_steps(h, 0, middle)
        beside(cuts[0], cuts[1])
        forward_steps(h, middle, groups)
        swap(h).start()
        beside(cuts[1], cuts[2])
        swap(h).wait()
        weigh(h)
        back_steps(h, 0, middle)
        beside(cuts[2], cuts[3])
        back_steps(h, middle, groups)

    pass_on(0, z, has_above, has_below)

    shape = table_vmem.shape
    place = lax.broadcasted_iota(jnp.int32, shape, 1) * row_blocks + lax.broadcasted_iota(jnp.int32, shape, 0)

    def table_step(s, table):
        pair = jnp.where(s < count_ref[0, 0, 0], cols_ref[0, 0, s] * row_blocks + rows_ref[0, 0, s], -1)
        return jnp.where(place == pair, s, table)

    table_vmem[...] = lax.fori_loop(0, slots, table_step, jnp.full(shape, slots, jnp.int32))
    table_copy = pltpu.make_async_copy(table_vmem, table_ref, table_sem)
    table_copy.start()
    for h in range(parts):
        terms[h, slots] = jnp.zeros((probes, ts), jnp.float32)
        forward[h] = jnp.zeros(forward.shape[1:], jnp.float32)

    turns = [1 + min(lines - 1, (lines - 1) * i * 4 // (3 * chunks)) for i in range(chunks + 1)]

    for i in range(chunks):
        tile_copy(i).wait()

        def turn_step(n, carry):
            for u in range(2):
                s = i * per_chunk + n * 2 + u
                turned[s] = tiles[s].T
            return carry

        lax.fori_loop(0, per_chunk // 2, turn_step, 0)
        gather_steps(0, turns[i], turns[i + 1])
        if turns[i] < turns[i + 1] == lines:
            pass_on(1, z, has_above, has_below)
    table_copy.wait()
    gather_end(0)
    for h in range(parts):
        compute(h, functools.partial(gather_steps, 1) if h == 0 else lambda first, last: None)
        y_all(h)
        if h == 0:
            gather_end(1)
    for i in range(3):
        z_steps(0, cuts[i], cuts[i + 1])
        z_steps(1, cuts[i], cuts[i + 1])
    finish(0)
    finish(1)
    z_end(0)
    z_end(1)


def on_device(row_devices, probes, tile_data, tile_rows, tile_cols, tile_count, active):
    tiles = tile_data[0, 0]
    slots, ts = tiles.shape[0], tiles.shape[1]
    probe_count, owned = probes.shape[1], probes.shape[2]
    blocks = owned // ts
    col_blocks = row_devices * blocks
    row_blocks = active.shape[0] // ts
    lines = row_devices // 2
    chunks = 8 if slots % 16 == 0 else 1
    unroll = 16 if slots % 16 == 0 else 1
    parts = 2
    share = probe_count // parts

    smem = pl.BlockSpec(memory_space=pltpu.SMEM)
    vmem = pl.BlockSpec(memory_space=pltpu.VMEM)
    f32, bf16, dma = jnp.float32, jnp.bfloat16, pltpu.SemaphoreType.DMA
    message = (2 * blocks + 1, share, ts // 2)
    back = pl.pallas_call(
        functools.partial(kernel, lines, row_blocks, blocks, chunks, unroll, parts),
        out_shape=jax.ShapeDtypeStruct((probe_count, owned), f32),
        in_specs=[smem, smem, smem, vmem, vmem, pl.BlockSpec(memory_space=pl.ANY)],
        out_specs=vmem,
        scratch_shapes=[
            pltpu.VMEM(tiles.shape, bf16),
            pltpu.VMEM(tiles.shape, bf16),
            pltpu.VMEM((col_blocks, share, ts), bf16),
            pltpu.VMEM((col_blocks, share, ts), bf16),
            pltpu.VMEM((parts, row_blocks * share, ts), f32),
            pltpu.VMEM((parts, row_blocks * share, ts), f32),
            pltpu.VMEM((parts, row_blocks, share, ts), bf16),
            pltpu.VMEM((parts, slots + 1, share, ts), f32),
            pltpu.VMEM((blocks, share, ts), f32),
            pltpu.VMEM((parts, lines, blocks, share, ts), f32),
            pltpu.VMEM((parts, lines) + message, jnp.int16),
            pltpu.VMEM((parts, lines) + message, jnp.int16),
            pltpu.VMEM((parts, lines) + message, jnp.int16),
            pltpu.VMEM((parts, lines + 1) + message, jnp.int16),
            pltpu.VMEM((row_blocks, col_blocks), jnp.int32),
            pltpu.SMEM((row_blocks, col_blocks), jnp.int32),
            dma((chunks,)), dma,
            dma((parts, lines)), dma((parts, lines)), dma((parts, lines)), dma((parts, row_devices)),
            dma((parts,)), dma((parts,)),
            dma((parts, lines)), dma((parts, lines)), dma((parts, lines)), dma((parts, lines + 1)),
        ],
        compiler_params=pltpu.CompilerParams(
            collective_id=0, has_side_effects=True, vmem_limit_bytes=56 * 1024 * 1024
        ),
        cost_estimate=pl.CostEstimate(
            flops=2 * slots * ts * ts * probe_count * (row_blocks + 1),
            bytes_accessed=2 * tiles.size, transcendentals=0,
        ),
    )(
        tile_cols, tile_rows, tile_count,
        probes[0], active.reshape(row_blocks * 2, ts // 2), tiles,
    )
    return (probes[0].astype(f32) + back)[None]


def solution(mesh):
    placed = (
        P(("groups", "col"), None, "row"),
        P(("groups", "row"), "col", None, None, None),
        P(("groups", "row"), "col", None),
        P(("groups", "row"), "col", None),
        P(("groups", "row"), "col", None),
        P(("groups", "row")),
    )
    return jax.shard_map(
        functools.partial(on_device, mesh.shape["row"]),
        mesh=mesh,
        in_specs=placed,
        out_specs=P(("groups", "col"), None, "row"),
        check_vma=False,
    )
```
